32 devices in a mesh: tm: 8 (over y, x, core), ops: 4 (over z).
Axes of the slice: x: 2, y: 2, z: 4, core: 2. Of those that a mesh axis runs over, the one named last changes fastest.
Arguments:
- node_blocks: bfloat16 [128, 384, 768], P(('tm', 'ops')), may hold values from -6 to 6
- first_pulls: int32 [32, 16], replicated, may hold values from 0 to 127, as said below
- first_left: int32 [32, 24], replicated, may hold values from 0 to 15
- first_right: int32 [32, 24], replicated, may hold values from 0 to 15
- first_live: int32 [32], replicated, may hold values from 1 to 24, as said below
- second_pulls: int32 [32, 16], replicated, may hold values from 0 to 767, as said below
- second_left: int32 [32, 16], replicated, may hold values from 0 to 15
- second_right: int32 [32, 16], replicated, may hold values from 0 to 15
- second_live: int32 [32], replicated, may hold values from 1 to 16, as said below
- diagram_ids: int32 [32, 16], replicated, may hold values from 0 to 31, as said below
- diagram_signs: int32 [32, 16], replicated, may hold values from -1 to 1, as said below
Outputs:
- diagrams: float32 [32, 384, 768], P(('tm', 'ops'))
The draws below stay inside these ranges and needn't reach their ends.
Inputs may be any that keep to these rules, and one draw needn't show every extreme that they name: `first_pulls`: every node in row w belongs to a device with the same ops index as w. At most 2 entries of a row belong to any one device, and every row has a device with exactly 2. `first_live`: some worker has 24 pairs. `second_pulls`: each entry is an id h * 24 + p with p < first_live[h], where h is a device with the same tm index as w. At most 4 entries of a row belong to any one device h, and every row has a device with exactly 4. `second_live`: some worker has 16 pairs. `diagram_ids`: every diagram of row w is owned by a device with the same tm index as w. `diagram_signs`: each entry is +1 or -1.
All inputs are finite; a program needn't handle non-finite values.
Results may differ from the reference program's by a relative error of at most 0.004.
Values may be sent and summed in bfloat16 or wider, within the bound.
A program may use at most 128 MiB of HBM per device.

```python
import math
import jax
import jax.numpy as jnp
from jax import lax

R = 384
NODE_DEV = 4
INP1 = 16
CAP1 = 24
INP2 = 16
CAP2 = 16
DIAG_DEV = 1
NODES = 128
DIAGS = 32
N_TM = 8
N_OPS = 4


def skewed_counts(key, top_count):
    worker_count = N_TM * N_OPS
    lower = jax.random.randint(jax.random.fold_in(key, 1), (worker_count,), 0, top_count)
    higher = jax.random.randint(jax.random.fold_in(key, 2), (worker_count,), 0, top_count)
    counts = 1 + jnp.minimum(lower, higher)
    busiest = jax.random.randint(jax.random.fold_in(key, 3), (), 0, worker_count)
    return jnp.where(jnp.arange(worker_count) == busiest, top_count, counts).astype(jnp.int32)


def first_counts(key):
    return skewed_counts(jax.random.fold_in(key, 101), CAP1)


def row_orders(key, length, reads):
    worker_count = N_TM * N_OPS
    row_keys = jax.random.split(key, worker_count)

    def one_row(row_key):
        return jax.random.permutation(row_key, length)
    orders = jax.vmap(one_row)(row_keys)
    return orders[:, jnp.arange(reads) % length]


def row_starts():
    worker_count = N_TM * N_OPS
    return (jnp.arange(worker_count) // N_OPS * N_OPS)[:, None]


def draw_first_pulls(key, part):
    worker_count = N_TM * N_OPS
    source_times = row_orders(jax.random.fold_in(key, 201), N_TM, INP1)
    node_slot = jax.random.randint(jax.random.fold_in(key, 202), (worker_count, INP1), 0, NODE_DEV)
    groups = (jnp.arange(worker_count) % N_OPS)[:, None]
    return ((source_times * N_OPS + groups) * NODE_DEV + node_slot).astype(jnp.int32)


def draw_first_left(key, part):
    return jax.random.randint(jax.random.fold_in(key, 203), (N_TM * N_OPS, CAP1), 0, INP1).astype(jnp.int32)


def draw_first_right(key, part):
    return jax.random.randint(jax.random.fold_in(key, 204), (N_TM * N_OPS, CAP1), 0, INP1).astype(jnp.int32)


def draw_first_live(key, part):
    return first_counts(key)


def draw_second_pulls(key, part):
    worker_count = N_TM * N_OPS
    counts = first_counts(key)
    source_groups = row_orders(jax.random.fold_in(key, 301), N_OPS, INP2)
    holders = row_starts() + source_groups
    raw_draws = jax.random.randint(jax.random.fold_in(key, 302), (worker_count, INP2), 0, 1 << 20)
    slot_draws = raw_draws % jnp.take(counts, holders)
    return (holders * CAP1 + slot_draws).astype(jnp.int32)


def draw_second_left(key, part):
    return jax.random.randint(jax.random.fold_in(key, 303), (N_TM * N_OPS, CAP2), 0, INP2).astype(jnp.int32)


def draw_second_right(key, part):
    return jax.random.randint(jax.random.fold_in(key, 304), (N_TM * N_OPS, CAP2), 0, INP2).astype(jnp.int32)


def draw_second_live(key, part):
    return skewed_counts(jax.random.fold_in(key, 401), CAP2)


def draw_diagram_ids(key, part):
    worker_count = N_TM * N_OPS
    groups = jax.random.randint(jax.random.fold_in(key, 501), (worker_count, CAP2), 0, N_OPS)
    within = jax.random.randint(jax.random.fold_in(key, 502), (worker_count, CAP2), 0, DIAG_DEV)
    return ((row_starts() + groups) * DIAG_DEV + within).astype(jnp.int32)


def draw_diagram_signs(key, part):
    coins = jax.random.randint(jax.random.fold_in(key, 601), (N_TM * N_OPS, CAP2), 0, 2)
    return (coins * 2 - 1).astype(jnp.int32)


def level_of(rng, extent, pieces, low, top_value):
    loudness, own = 1.0, jax.random.fold_in(rng, 6)
    for position, blocks in pieces:
        steps = jnp.exp(jax.random.uniform(jax.random.fold_in(own, position), (blocks,), jnp.float32, low / len(pieces), top_value / len(pieces)))
        loudness = loudness * jnp.repeat(steps, extent[position] // blocks).reshape([-1 if axis == position else 1 for axis in range(len(extent))])
    return loudness


def gaussian(key, extent, deviation, limit, shards=(), kind=jnp.bfloat16):
    drawn = jax.random.normal(key, extent, jnp.float32) * deviation
    if len(shards) > 0:
        drawn = level_of(key, extent, shards, -0.22, 0.18) * drawn
    return jnp.clip(drawn, min=-limit, max=limit).astype(kind)


def setup_inputs(seed: int = 0) -> dict:
    streams_of = jax.random.split(jax.random.key(seed), 12)
    return {
        "node_blocks": gaussian(streams_of[0], (NODES, R, 2 * R), 1.0, 6.0, ((0, 32),)),
        "first_pulls": draw_first_pulls(jax.random.fold_in(streams_of[11], 71), 0),
        "first_left": draw_first_left(jax.random.fold_in(streams_of[11], 71), 0),
        "first_right": draw_first_right(jax.random.fold_in(streams_of[11], 71), 0),
        "first_live": draw_first_live(jax.random.fold_in(streams_of[11], 71), 0),
        "second_pulls": draw_second_pulls(jax.random.fold_in(streams_of[11], 71), 0),
        "second_left": draw_second_left(jax.random.fold_in(streams_of[11], 71), 0),
        "second_right": draw_second_right(jax.random.fold_in(streams_of[11], 71), 0),
        "second_live": draw_second_live(jax.random.fold_in(streams_of[11], 71), 0),
        "diagram_ids": draw_diagram_ids(jax.random.fold_in(streams_of[11], 71), 0),
        "diagram_signs": draw_diagram_signs(jax.random.fold_in(streams_of[11], 71), 0),
    }


def complex_product(first_block, second_block):
    first_block = first_block.astype(jnp.float32)
    second_block = second_block.astype(jnp.float32)
    rank_size = first_block.shape[0]
    second_real = second_block[:, :rank_size]
    second_imag = second_block[:, rank_size:]
    upper_half = jnp.concatenate([second_real, second_imag], axis=1)
    lower_half = jnp.concatenate([-second_imag, second_real], axis=1)
    stacked = jnp.concatenate([upper_half, lower_half], axis=0)
    return jnp.dot(first_block, stacked, precision=lax.Precision.HIGHEST, preferred_element_type=jnp.float32)

def reference(node_blocks, first_pulls, first_left, first_right, first_live, second_pulls, second_left, second_right, second_live, diagram_ids, diagram_signs):
    rank_size = node_blocks.shape[1]
    norm_factor = 1.0 / math.sqrt(2.0 * rank_size)
    block_shape = (rank_size, 2 * rank_size)

    def first_worker(worker):
        pull_list = first_pulls[worker]
        live_count = first_live[worker]

        def first_pair(pair_index):
            first_block = node_blocks[pull_list[first_left[worker, pair_index]]]
            second_block = node_blocks[pull_list[first_right[worker, pair_index]]]
            live_mask = (pair_index < live_count).astype(jnp.float32)
            return (complex_product(first_block, second_block) * (norm_factor * live_mask)).astype(jnp.bfloat16)
        return lax.map(first_pair, jnp.arange(CAP1, dtype=jnp.int32))

    def time_row(time_row_index):
        row_workers = (time_row_index * N_OPS + jnp.arange(N_OPS)).astype(jnp.int32)
        stored = lax.map(first_worker, row_workers).reshape((N_OPS * CAP1,) + block_shape)
        row_base = time_row_index * N_OPS * CAP1
        pair_workers = jnp.repeat(row_workers, CAP2)
        pair_slots = jnp.tile(jnp.arange(CAP2, dtype=jnp.int32), N_OPS)

        def second_pair(diagram_total, pair_info):
            worker, slot_index = pair_info
            pull_list = second_pulls[worker] - row_base
            first_block = stored[pull_list[second_left[worker, slot_index]]]
            second_block = stored[pull_list[second_right[worker, slot_index]]]
            live_mask = (slot_index < second_live[worker]).astype(jnp.float32)
            weight = diagram_signs[worker, slot_index].astype(jnp.float32) * live_mask
            signed_term = complex_product(first_block, second_block) * norm_factor * weight
            target = diagram_ids[worker, slot_index] - time_row_index * N_OPS * DIAG_DEV
            return (diagram_total.at[target].add(signed_term), None)
        result = lax.scan(second_pair, jnp.zeros((N_OPS * DIAG_DEV,) + block_shape, jnp.float32), (pair_workers, pair_slots))
        return result[0]
    per_row = lax.map(time_row, jnp.arange(N_TM, dtype=jnp.int32))
    return per_row.reshape((DIAGS,) + block_shape)
```

```python
import math

import jax
import jax.numpy as jnp
from jax import lax
from jax.experimental import pallas as pl
from jax.experimental.pallas import tpu as pltpu
from jax.sharding import PartitionSpec as P

DIAG_DEV = 1
VMEM_BYTES = 48 * 1024 * 1024


def complex_product(first_block, second_block, stacked):
    rank_size = first_block.shape[0]
    stacked[:rank_size, :] = second_block
    stacked[rank_size:, :rank_size] = -second_block[:, rank_size:]
    stacked[rank_size:, rank_size:] = second_block[:, :rank_size]
    return jnp.dot(first_block, stacked[...], preferred_element_type=jnp.float32)


def first_kernel(norm_factor, left, right, used, a_ref, b_ref, out_ref, stacked):
    @pl.when(used[pl.program_id(0)] > 0)
    def _():
        product = complex_product(a_ref[0], b_ref[0], stacked)
        out_ref[0] = (product * norm_factor).astype(out_ref.dtype)


def second_kernel(left, right, target, sign, live, norm, a_ref, b_ref, out_ref, total, stacked):
    step = pl.program_id(0)

    @pl.when(step == 0)
    def _():
        total[...] = jnp.zeros_like(total)

    @pl.when(step < live[0])
    def _():
        weight = sign[step].astype(jnp.float32) * norm
        total[target[step]] += complex_product(a_ref[0], b_ref[0], stacked) * weight

    @pl.when(step == pl.num_programs(0) - 1)
    def _():
        out_ref[...] = total[...].astype(out_ref.dtype)


def pair_specs(rank_size):
    block = (1, rank_size, 2 * rank_size)
    return [
        pl.BlockSpec(block, lambda s, left, right, *_: (left[s], 0, 0)),
        pl.BlockSpec(block, lambda s, left, right, *_: (right[s], 0, 0)),
    ]


def first_products(blocks, left, right, used, norm_factor):
    steps = left.shape[0]
    rank_size = blocks.shape[1]
    block = (1, rank_size, 2 * rank_size)
    return pl.pallas_call(
        lambda *refs: first_kernel(norm_factor, *refs),
        grid_spec=pltpu.PrefetchScalarGridSpec(
            num_scalar_prefetch=3,
            grid=(steps,),
            in_specs=pair_specs(rank_size),
            out_specs=pl.BlockSpec(block, lambda s, *_: (s, 0, 0)),
            scratch_shapes=[pltpu.VMEM((2 * rank_size, 2 * rank_size), jnp.bfloat16)],
        ),
        out_shape=jax.ShapeDtypeStruct((steps,) + block[1:], jnp.bfloat16),
        compiler_params=pltpu.CompilerParams(vmem_limit_bytes=VMEM_BYTES),
        name="first_section",
    )(left, right, used, blocks, blocks)


def second_sums(blocks, left, right, target, sign, live, norm_factor, diagram_count):
    steps = left.shape[0]
    rank_size = blocks.shape[1]
    shape = (diagram_count, rank_size, 2 * rank_size)
    return pl.pallas_call(
        lambda left, right, target, sign, live, *refs: second_kernel(
            left, right, target, sign, live, norm_factor, *refs
        ),
        grid_spec=pltpu.PrefetchScalarGridSpec(
            num_scalar_prefetch=5,
            grid=(steps,),
            in_specs=pair_specs(rank_size),
            out_specs=pl.BlockSpec(shape, lambda s, *_: (0, 0, 0)),
            scratch_shapes=[
                pltpu.VMEM(shape, jnp.float32),
                pltpu.VMEM((2 * rank_size, 2 * rank_size), jnp.bfloat16),
            ],
        ),
        out_shape=jax.ShapeDtypeStruct(shape, jnp.bfloat16),
        compiler_params=pltpu.CompilerParams(vmem_limit_bytes=VMEM_BYTES),
        name="second_section",
    )(left, right, target, sign, live, blocks, blocks)


def source_ranks(sources):
    length = sources.shape[-1]
    positions = jnp.arange(length)
    earlier = positions[:, None] > positions[None, :]
    same_source = sources[..., :, None] == sources[..., None, :]
    return jnp.sum(jnp.logical_and(same_source, earlier), axis=-1)


def pick(table, index):
    match = index[..., None] == jnp.arange(table.shape[0])
    return jnp.sum(jnp.where(match, table, 0), axis=-1)


def body(
    node_blocks,
    first_pulls,
    first_left,
    first_right,
    first_live,
    second_pulls,
    second_left,
    second_right,
    second_live,
    diagram_ids,
    diagram_signs,
):
    group_count = lax.axis_size("ops")
    time_index = lax.axis_index("tm")
    group_index = lax.axis_index("ops")
    worker = time_index * group_count + group_index
    held_nodes = node_blocks.shape[0]
    rank_size = node_blocks.shape[1]
    norm_factor = 1.0 / math.sqrt(2.0 * rank_size)
    first_cap = first_left.shape[1]
    second_reads = second_pulls.shape[1]
    second_cap = second_left.shape[1]
    second_slots = max(1, second_reads // group_count)

    shard_rows = lax.all_gather(node_blocks, "tm", axis=0, tiled=True)

    def own_rows(table):
        return lax.dynamic_slice_in_dim(table, time_index * group_count, group_count, 0)

    own_pulls = first_pulls[worker]
    column_pos = own_pulls // held_nodes // group_count * held_nodes + own_pulls % held_nodes
    row_pulls = own_rows(second_pulls)
    row_sources = row_pulls // first_cap % group_count
    ranks = source_ranks(row_sources)
    from_here = jnp.logical_and(
        (row_sources == group_index)[:, None, :],
        ranks[:, None, :] == jnp.arange(second_slots)[None, :, None],
    )
    pair_ids = jnp.sum(jnp.where(from_here, (row_pulls % first_cap)[:, None, :], 0), axis=-1)
    live = jnp.arange(second_cap)[None, :] < own_rows(second_live)[:, None]
    spots = jnp.arange(second_reads)[None, None, :]
    read = jnp.logical_or(
        own_rows(second_left)[:, :, None] == spots, own_rows(second_right)[:, :, None] == spots
    )
    read = jnp.any(jnp.logical_and(read, live[:, :, None]), axis=1)
    used = jnp.any(jnp.logical_and(from_here, read[:, None, :]), axis=-1)
    pair_ids = pair_ids.reshape(-1)
    left_nodes = pick(column_pos, pick(first_left[worker], pair_ids))
    right_nodes = pick(column_pos, pick(first_right[worker], pair_ids))
    own_sources = lax.dynamic_index_in_dim(row_sources, group_index, 0, keepdims=False)
    own_ranks = lax.dynamic_index_in_dim(ranks, group_index, 0, keepdims=False)
    places = own_sources * second_slots + own_ranks
    second_left_at = pick(places, second_left[worker])
    second_right_at = pick(places, second_right[worker])
    targets = diagram_ids[worker] - time_index * group_count * DIAG_DEV

    outgoing = first_products(
        shard_rows, left_nodes, right_nodes, used.reshape(-1).astype(jnp.int32), norm_factor
    )
    arrived = lax.all_to_all(outgoing, "ops", split_axis=0, concat_axis=0, tiled=True)
    partial_sum = second_sums(
        arrived,
        second_left_at,
        second_right_at,
        targets,
        diagram_signs[worker],
        second_live[worker][None],
        norm_factor,
        group_count * DIAG_DEV,
    )
    terms = lax.all_to_all(partial_sum, "ops", split_axis=0, concat_axis=0, tiled=True)
    terms = terms.reshape((group_count, DIAG_DEV) + terms.shape[1:])
    return jnp.sum(terms.astype(jnp.float32), axis=0)


def solution(mesh):
    placed = (P(("tm", "ops"), None, None), P(), P(), P(), P(), P(), P(), P(), P(), P(), P())
    return jax.shard_map(
        body, mesh=mesh, in_specs=placed, out_specs=P(("tm", "ops"), None, None), check_vma=False
    )
```

```python
import math

import jax
import jax.numpy as jnp
from jax import lax
from jax.experimental import pallas as pl
from jax.experimental.pallas import tpu as pltpu
from jax.sharding import PartitionSpec as P

DIAG_DEV = 1
VMEM_BYTES = 48 * 1024 * 1024


def complex_product(first_block, second_block, stacked):
    rank_size = first_block.shape[0]
    stacked[:rank_size, :] = second_block
    stacked[rank_size:, :rank_size] = -second_block[:, rank_size:]
    stacked[rank_size:, rank_size:] = second_block[:, :rank_size]
    return jnp.dot(first_block, stacked[...], preferred_element_type=jnp.float32)


def first_kernel(norm_factor, left, right, used, a_ref, b_ref, out_ref, stacked):
    @pl.when(used[pl.program_id(0)] > 0)
    def _():
        product = complex_product(a_ref[0], b_ref[0], stacked)
        out_ref[0] = (product * norm_factor).astype(out_ref.dtype)


def second_kernel(region_count, norm, left, right, target, sign, live, *refs):
    regions = refs[:region_count]
    out_ref, held, total, stacked, arrivals = refs[region_count:]
    slots = regions[0].shape[0]
    copies = [
        pltpu.make_async_copy(regions[k], held.at[pl.ds(k * slots, slots)], arrivals.at[k])
        for k in range(region_count)
    ]
    for copy in copies:
        copy.start()
    total[...] = jnp.zeros_like(total)
    for copy in copies:
        copy.wait()

    @pl.loop(0, live[0])
    def _(step):
        weight = sign[step].astype(jnp.float32) * norm
        product = complex_product(held[left[step]], held[right[step]], stacked)
        total[target[step]] += product * weight

    out_ref[...] = total[...].astype(out_ref.dtype)


def product_cost(count, rank_size):
    return pl.CostEstimate(
        flops=16 * count * rank_size**3 // 2,
        bytes_accessed=12 * count * rank_size**2,
        transcendentals=0,
    )


def first_products(blocks, left, right, used, norm_factor):
    steps = left.shape[0]
    rank_size = blocks.shape[1]
    block = (1, rank_size, 2 * rank_size)
    return pl.pallas_call(
        lambda *refs: first_kernel(norm_factor, *refs),
        grid_spec=pltpu.PrefetchScalarGridSpec(
            num_scalar_prefetch=3,
            grid=(steps,),
            in_specs=[
                pl.BlockSpec(block, lambda s, left, right, used: (left[s], 0, 0)),
                pl.BlockSpec(block, lambda s, left, right, used: (right[s], 0, 0)),
            ],
            out_specs=pl.BlockSpec(block, lambda s, *_: (s, 0, 0)),
            scratch_shapes=[pltpu.VMEM((2 * rank_size, 2 * rank_size), jnp.bfloat16)],
        ),
        out_shape=jax.ShapeDtypeStruct((steps,) + block[1:], jnp.bfloat16),
        compiler_params=pltpu.CompilerParams(vmem_limit_bytes=VMEM_BYTES),
        cost_estimate=product_cost(steps, rank_size),
        name="first_section",
    )(left, right, used, blocks, blocks)


def second_sums(regions, left, right, target, sign, live, norm_factor, diagram_count):
    steps = left.shape[0]
    slots, rank_size, width = regions[0].shape
    shape = (diagram_count, rank_size, width)
    return pl.pallas_call(
        lambda *refs: second_kernel(len(regions), norm_factor, *refs),
        in_specs=[pl.BlockSpec(memory_space=pltpu.SMEM)] * 5
        + [pl.BlockSpec(memory_space=pl.ANY)] * len(regions),
        out_specs=pl.BlockSpec(memory_space=pltpu.VMEM),
        scratch_shapes=[
            pltpu.VMEM((len(regions) * slots, rank_size, width), jnp.bfloat16),
            pltpu.VMEM(shape, jnp.float32),
            pltpu.VMEM((2 * rank_size, width), jnp.bfloat16),
            pltpu.SemaphoreType.DMA((len(regions),)),
        ],
        out_shape=jax.ShapeDtypeStruct(shape, jnp.bfloat16),
        compiler_params=pltpu.CompilerParams(vmem_limit_bytes=VMEM_BYTES),
        cost_estimate=product_cost(steps, rank_size),
        name="second_section",
    )(left, right, target, sign, live, *regions)


def source_ranks(sources):
    length = sources.shape[-1]
    positions = jnp.arange(length)
    earlier = positions[:, None] > positions[None, :]
    same_source = sources[..., :, None] == sources[..., None, :]
    return jnp.sum(jnp.logical_and(same_source, earlier), axis=-1)


def pick(table, index):
    match = index[..., None] == jnp.arange(table.shape[0])
    return jnp.sum(jnp.where(match, table, 0), axis=-1)


def body(
    node_blocks,
    first_pulls,
    first_left,
    first_right,
    first_live,
    second_pulls,
    second_left,
    second_right,
    second_live,
    diagram_ids,
    diagram_signs,
):
    group_count = lax.axis_size("ops")
    time_index = lax.axis_index("tm")
    group_index = lax.axis_index("ops")
    worker = time_index * group_count + group_index
    held_nodes = node_blocks.shape[0]
    rank_size = node_blocks.shape[1]
    norm_factor = 1.0 / math.sqrt(2.0 * rank_size)
    first_cap = first_left.shape[1]
    second_reads = second_pulls.shape[1]
    second_cap = second_left.shape[1]
    second_slots = max(1, second_reads // group_count)
    half = group_count // 2

    def far_of(group):
        return 0 if group >= half else group_count - 1

    far_index = jnp.where(group_index >= half, 0, group_count - 1)
    near_rows = lax.all_gather(node_blocks, "tm", axis=0, tiled=True)
    far_nodes = None
    for step in range(half):
        crossing = [(0, half + step), (group_count - 1, half - 1 - step)]
        came = lax.ppermute(node_blocks, "ops", crossing)
        takes = jnp.logical_or(group_index == half + step, group_index == half - 1 - step)
        far_nodes = came if far_nodes is None else jnp.where(takes, came, far_nodes)
    far_rows = lax.all_gather(far_nodes, "tm", axis=0, tiled=True)

    def own_rows(table):
        return lax.dynamic_slice_in_dim(table, time_index * group_count, group_count, 0)

    def turned(rows):
        return lax.dynamic_slice_in_dim(
            jnp.concatenate([rows, rows], axis=0), group_index, group_count, 0
        )

    row_start = time_index * group_count
    row_pulls = own_rows(second_pulls)
    row_sources = row_pulls // first_cap % group_count
    row_pairs = row_pulls % first_cap
    ranks = source_ranks(row_sources)
    live = jnp.arange(second_cap)[None, :] < own_rows(second_live)[:, None]
    spots = jnp.arange(second_reads)[None, None, :]
    read = jnp.logical_or(
        own_rows(second_left)[:, :, None] == spots, own_rows(second_right)[:, :, None] == spots
    )
    read = jnp.any(jnp.logical_and(read, live[:, :, None]), axis=1)
    slot_ids = jnp.arange(second_slots)[None, :, None]

    def slots_of(sources, source, pairs, slot_ranks, reads):
        chosen = jnp.logical_and((sources == source)[:, None, :], slot_ranks[:, None, :] == slot_ids)
        pair_ids = jnp.sum(jnp.where(chosen, pairs[:, None, :], 0), axis=-1)
        used = jnp.any(jnp.logical_and(chosen, reads[:, None, :]), axis=-1)
        return pair_ids, used.astype(jnp.int32)

    def factors(holder, pair_ids):
        pulls = first_pulls[holder]
        column_pos = pulls // held_nodes // group_count * held_nodes + pulls % held_nodes
        return (
            pick(column_pos, pick(first_left[holder], pair_ids)),
            pick(column_pos, pick(first_right[holder], pair_ids)),
        )

    pair_ids, used = slots_of(
        turned(row_sources), group_index, turned(row_pairs), turned(ranks), turned(read)
    )
    readers = (group_index + jnp.arange(group_count)) % group_count
    apart = jnp.where(readers >= half, 0, group_count - 1) == group_index
    used = jnp.where(apart[:, None], 0, used)
    left_nodes, right_nodes = factors(worker, pair_ids)

    def own_row(rows):
        return lax.dynamic_slice_in_dim(rows, group_index, 1, 0)

    own_sources = own_row(row_sources)
    far_ids, far_used = slots_of(
        own_sources, far_index, own_row(row_pairs), own_row(ranks), own_row(read)
    )
    far_left, far_right = factors(row_start + far_index, far_ids)
    region = jnp.where(
        own_sources == far_index,
        group_count,
        (group_index - own_sources + group_count) % group_count,
    )
    places = (region * second_slots + own_row(ranks))[0]
    second_left_at = pick(places, second_left[worker])
    second_right_at = pick(places, second_right[worker])
    targets = diagram_ids[worker] - row_start * DIAG_DEV

    def near_products(turn):
        return first_products(
            near_rows, left_nodes[turn], right_nodes[turn], used[turn], norm_factor
        )

    regions = [None] * (group_count + 1)
    for turn in sorted(range(1, group_count), key=lambda j: -min(j, group_count - j)):
        pairs = [
            (source, (source + turn) % group_count)
            for source in range(group_count)
            if far_of((source + turn) % group_count) != source
        ]
        if pairs:
            regions[turn] = lax.ppermute(near_products(turn), "ops", pairs)
    regions[0] = near_products(0)
    regions[group_count] = first_products(
        far_rows, far_left[0], far_right[0], far_used[0], norm_factor
    )
    regions = [regions[0] if block is None else block for block in regions]
    partial_sum = second_sums(
        regions,
        second_left_at,
        second_right_at,
        targets,
        diagram_signs[worker],
        second_live[worker][None],
        norm_factor,
        group_count * DIAG_DEV,
    )
    terms = lax.all_to_all(partial_sum, "ops", split_axis=0, concat_axis=0, tiled=True)
    terms = terms.reshape((group_count, DIAG_DEV) + terms.shape[1:])
    return jnp.sum(terms.astype(jnp.float32), axis=0)


def solution(mesh):
    placed = (P(("tm", "ops"), None, None), P(), P(), P(), P(), P(), P(), P(), P(), P(), P())
    return jax.shard_map(
        body, mesh=mesh, in_specs=placed, out_specs=P(("tm", "ops"), None, None), check_vma=False
    )
```

```python
import math

import jax
import jax.numpy as jnp
from jax import lax
from jax.experimental import pallas as pl
from jax.experimental.pallas import tpu as pltpu
from jax.sharding import PartitionSpec as P

DIAG_DEV = 1
VMEM_BYTES = 48 * 1024 * 1024


def complex_product(first_block, second_block, stacked):
    rank_size = first_block.shape[0]
    stacked[:rank_size, :] = second_block
    stacked[rank_size:, :rank_size] = -second_block[:, rank_size:]
    stacked[rank_size:, rank_size:] = second_block[:, :rank_size]
    return jnp.dot(first_block, stacked[...], preferred_element_type=jnp.float32)


def first_kernel(norm_factor, left, right, used, a_ref, b_ref, out_ref, stacked):
    @pl.when(used[pl.program_id(0)] > 0)
    def _():
        product = complex_product(a_ref[0], b_ref[0], stacked)
        out_ref[0] = (product * norm_factor).astype(out_ref.dtype)


def second_kernel(region_count, norm, left, right, target, sign, live, *refs):
    regions = refs[:region_count]
    out_ref, held, total, stacked, arrivals = refs[region_count:]
    slots = regions[0].shape[0]
    copies = [
        pltpu.make_async_copy(regions[k], held.at[pl.ds(k * slots, slots)], arrivals.at[k])
        for k in range(region_count)
    ]
    for copy in copies:
        copy.start()
    total[...] = jnp.zeros_like(total)
    for copy in copies:
        copy.wait()

    @pl.loop(0, live[0])
    def _(step):
        weight = sign[step].astype(jnp.float32) * norm
        product = complex_product(held[left[step]], held[right[step]], stacked)
        total[target[step]] += product * weight

    out_ref[...] = total[...].astype(out_ref.dtype)


def product_cost(count, rank_size):
    return pl.CostEstimate(
        flops=16 * count * rank_size**3 // 2,
        bytes_accessed=12 * count * rank_size**2,
        transcendentals=0,
    )


def first_products(blocks, left, right, used, norm_factor):
    steps = left.shape[0]
    rank_size = blocks.shape[1]
    block = (1, rank_size, 2 * rank_size)
    return pl.pallas_call(
        lambda *refs: first_kernel(norm_factor, *refs),
        grid_spec=pltpu.PrefetchScalarGridSpec(
            num_scalar_prefetch=3,
            grid=(steps,),
            in_specs=[
                pl.BlockSpec(block, lambda s, left, right, used: (left[s], 0, 0)),
                pl.BlockSpec(block, lambda s, left, right, used: (right[s], 0, 0)),
            ],
            out_specs=pl.BlockSpec(block, lambda s, *_: (s, 0, 0)),
            scratch_shapes=[pltpu.VMEM((2 * rank_size, 2 * rank_size), jnp.bfloat16)],
        ),
        out_shape=jax.ShapeDtypeStruct((steps,) + block[1:], jnp.bfloat16),
        compiler_params=pltpu.CompilerParams(vmem_limit_bytes=VMEM_BYTES),
        cost_estimate=product_cost(steps, rank_size),
        name="first_section",
    )(left, right, used, blocks, blocks)


def second_sums(regions, left, right, target, sign, live, norm_factor, diagram_count):
    steps = left.shape[0]
    slots, rank_size, width = regions[0].shape
    shape = (diagram_count, rank_size, width)
    return pl.pallas_call(
        lambda *refs: second_kernel(len(regions), norm_factor, *refs),
        in_specs=[pl.BlockSpec(memory_space=pltpu.SMEM)] * 5
        + [pl.BlockSpec(memory_space=pl.ANY)] * len(regions),
        out_specs=pl.BlockSpec(memory_space=pltpu.VMEM),
        scratch_shapes=[
            pltpu.VMEM((len(regions) * slots, rank_size, width), jnp.bfloat16),
            pltpu.VMEM(shape, jnp.float32),
            pltpu.VMEM((2 * rank_size, width), jnp.bfloat16),
            pltpu.SemaphoreType.DMA((len(regions),)),
        ],
        out_shape=jax.ShapeDtypeStruct(shape, jnp.bfloat16),
        compiler_params=pltpu.CompilerParams(vmem_limit_bytes=VMEM_BYTES),
        cost_estimate=product_cost(steps, rank_size),
        name="second_section",
    )(left, right, target, sign, live, *regions)


def source_ranks(sources):
    length = sources.shape[-1]
    positions = jnp.arange(length)
    earlier = positions[:, None] > positions[None, :]
    same_source = sources[..., :, None] == sources[..., None, :]
    return jnp.sum(jnp.logical_and(same_source, earlier), axis=-1)


def pick(table, index):
    match = index[..., None] == jnp.arange(table.shape[0])
    return jnp.sum(jnp.where(match, table, 0), axis=-1)


def body(
    node_blocks,
    first_pulls,
    first_left,
    first_right,
    first_live,
    second_pulls,
    second_left,
    second_right,
    second_live,
    diagram_ids,
    diagram_signs,
):
    group_count = lax.axis_size("ops")
    time_index = lax.axis_index("tm")
    group_index = lax.axis_index("ops")
    worker = time_index * group_count + group_index
    held_nodes = node_blocks.shape[0]
    rank_size = node_blocks.shape[1]
    norm_factor = 1.0 / math.sqrt(2.0 * rank_size)
    first_cap = first_left.shape[1]
    second_reads = second_pulls.shape[1]
    second_cap = second_left.shape[1]
    second_slots = max(1, second_reads // group_count)
    half = group_count // 2

    def far_of(group):
        return 0 if group >= half else group_count - 1

    far_index = jnp.where(group_index >= half, 0, group_count - 1)
    near_rows = lax.all_gather(node_blocks, "tm", axis=0, tiled=True)
    cuts = 2 if held_nodes % 2 == 0 else 1
    pieces = jnp.split(node_blocks, cuts, axis=0)
    chains = [[] for _ in range(cuts)]
    for cut in range(cuts):
        came = lax.ppermute(pieces[cut], "ops", [(0, half), (group_count - 1, half - 1)])
        chains[cut].append(came)
    for step in range(1, half):
        onward = [(half + step - 1, half + step), (half - step, half - 1 - step)]
        for cut in range(cuts):
            chains[cut].append(lax.ppermute(chains[cut][-1], "ops", onward))
    hop = jnp.where(group_index >= half, group_index - half, half - 1 - group_index)

    def arrived_at(chain):
        block = chain[0]
        for step in range(1, half):
            block = jnp.where(hop == step, chain[step], block)
        return block

    far_nodes = jnp.concatenate([arrived_at(chain) for chain in chains], axis=0)
    far_rows = lax.all_gather(far_nodes, "tm", axis=0, tiled=True)

    def own_rows(table):
        return lax.dynamic_slice_in_dim(table, time_index * group_count, group_count, 0)

    def turned(rows):
        return lax.dynamic_slice_in_dim(
            jnp.concatenate([rows, rows], axis=0), group_index, group_count, 0
        )

    row_start = time_index * group_count
    row_pulls = own_rows(second_pulls)
    row_sources = row_pulls // first_cap % group_count
    row_pairs = row_pulls % first_cap
    ranks = source_ranks(row_sources)
    live = jnp.arange(second_cap)[None, :] < own_rows(second_live)[:, None]
    spots = jnp.arange(second_reads)[None, None, :]
    read = jnp.logical_or(
        own_rows(second_left)[:, :, None] == spots, own_rows(second_right)[:, :, None] == spots
    )
    read = jnp.any(jnp.logical_and(read, live[:, :, None]), axis=1)
    slot_ids = jnp.arange(second_slots)[None, :, None]

    def slots_of(sources, source, pairs, slot_ranks, reads):
        chosen = jnp.logical_and((sources == source)[:, None, :], slot_ranks[:, None, :] == slot_ids)
        pair_ids = jnp.sum(jnp.where(chosen, pairs[:, None, :], 0), axis=-1)
        used = jnp.any(jnp.logical_and(chosen, reads[:, None, :]), axis=-1)
        return pair_ids, used.astype(jnp.int32)

    def factors(holder, pair_ids):
        pulls = first_pulls[holder]
        column_pos = pulls // held_nodes // group_count * held_nodes + pulls % held_nodes
        return (
            pick(column_pos, pick(first_left[holder], pair_ids)),
            pick(column_pos, pick(first_right[holder], pair_ids)),
        )

    pair_ids, used = slots_of(
        turned(row_sources), group_index, turned(row_pairs), turned(ranks), turned(read)
    )
    readers = (group_index + jnp.arange(group_count)) % group_count
    apart = jnp.where(readers >= half, 0, group_count - 1) == group_index
    used = jnp.where(apart[:, None], 0, used)
    left_nodes, right_nodes = factors(worker, pair_ids)

    def own_row(rows):
        return lax.dynamic_slice_in_dim(rows, group_index, 1, 0)

    own_sources = own_row(row_sources)
    far_ids, far_used = slots_of(
        own_sources, far_index, own_row(row_pairs), own_row(ranks), own_row(read)
    )
    far_left, far_right = factors(row_start + far_index, far_ids)
    region = jnp.where(
        own_sources == far_index,
        group_count,
        (group_index - own_sources + group_count) % group_count,
    )
    places = (region * second_slots + own_row(ranks))[0]
    second_left_at = pick(places, second_left[worker])
    second_right_at = pick(places, second_right[worker])
    targets = diagram_ids[worker] - row_start * DIAG_DEV

    def near_products(turn):
        return first_products(
            near_rows, left_nodes[turn], right_nodes[turn], used[turn], norm_factor
        )

    regions = [None] * (group_count + 1)
    for turn in sorted(range(1, group_count), key=lambda j: -min(j, group_count - j)):
        pairs = [
            (source, (source + turn) % group_count)
            for source in range(group_count)
            if far_of((source + turn) % group_count) != source
        ]
        if pairs:
            regions[turn] = lax.ppermute(near_products(turn), "ops", pairs)
    regions[0] = near_products(0)
    regions[group_count] = first_products(
        far_rows, far_left[0], far_right[0], far_used[0], norm_factor
    )
    regions = [regions[0] if block is None else block for block in regions]
    partial_sum = second_sums(
        regions,
        second_left_at,
        second_right_at,
        targets,
        diagram_signs[worker],
        second_live[worker][None],
        norm_factor,
        group_count * DIAG_DEV,
    )
    terms = lax.all_to_all(partial_sum, "ops", split_axis=0, concat_axis=0, tiled=True)
    terms = terms.reshape((group_count, DIAG_DEV) + terms.shape[1:])
    return jnp.sum(terms.astype(jnp.float32), axis=0)


def solution(mesh):
    placed = (P(("tm", "ops"), None, None), P(), P(), P(), P(), P(), P(), P(), P(), P(), P())
    return jax.shard_map(
        body, mesh=mesh, in_specs=placed, out_specs=P(("tm", "ops"), None, None), check_vma=False
    )
```

```python
import math

import jax
import jax.numpy as jnp
from jax import lax
from jax.experimental import pallas as pl
from jax.experimental.pallas import tpu as pltpu
from jax.sharding import PartitionSpec as P

DIAG_DEV = 1
VMEM_BYTES = 48 * 1024 * 1024


def complex_product(first_block, second_block, stacked):
    rank_size = first_block.shape[0]
    stacked[:rank_size, :] = second_block
    stacked[rank_size:, :rank_size] = -second_block[:, rank_size:]
    stacked[rank_size:, rank_size:] = second_block[:, :rank_size]
    return jnp.dot(first_block, stacked[...], preferred_element_type=jnp.float32)


def first_kernel(norm_factor, left, right, used, a_ref, b_ref, out_ref, stacked):
    @pl.when(used[pl.program_id(0)] > 0)
    def _():
        product = complex_product(a_ref[0], b_ref[0], stacked)
        out_ref[0] = (product * norm_factor).astype(out_ref.dtype)


def second_kernel(region_count, norm, left, right, target, sign, live, *refs):
    regions = refs[:region_count]
    *out_refs, held, total, stacked, arrivals = refs[region_count:]
    slots = regions[0].shape[0]
    copies = [
        pltpu.make_async_copy(regions[k], held.at[pl.ds(k * slots, slots)], arrivals.at[k])
        for k in range(region_count)
    ]
    for copy in copies:
        copy.start()
    total[...] = jnp.zeros_like(total)
    for copy in copies:
        copy.wait()

    @pl.loop(0, live[0])
    def _(step):
        weight = sign[step].astype(jnp.float32) * norm
        product = complex_product(held[left[step]], held[right[step]], stacked)
        total[target[step]] += product * weight

    owned = total.shape[0] // len(out_refs)
    for k, out_ref in enumerate(out_refs):
        out_ref[...] = total[pl.ds(k * owned, owned)].astype(out_ref.dtype)


def product_cost(count, rank_size):
    return pl.CostEstimate(
        flops=16 * count * rank_size**3 // 2,
        bytes_accessed=12 * count * rank_size**2,
        transcendentals=0,
    )


def first_products(blocks, left, right, used, norm_factor):
    steps = left.shape[0]
    rank_size = blocks.shape[1]
    block = (1, rank_size, 2 * rank_size)
    return pl.pallas_call(
        lambda *refs: first_kernel(norm_factor, *refs),
        grid_spec=pltpu.PrefetchScalarGridSpec(
            num_scalar_prefetch=3,
            grid=(steps,),
            in_specs=[
                pl.BlockSpec(block, lambda s, left, right, used: (left[s], 0, 0)),
                pl.BlockSpec(block, lambda s, left, right, used: (right[s], 0, 0)),
            ],
            out_specs=pl.BlockSpec(block, lambda s, *_: (s, 0, 0)),
            scratch_shapes=[pltpu.VMEM((2 * rank_size, 2 * rank_size), jnp.bfloat16)],
        ),
        out_shape=jax.ShapeDtypeStruct((steps,) + block[1:], jnp.bfloat16),
        compiler_params=pltpu.CompilerParams(vmem_limit_bytes=VMEM_BYTES),
        cost_estimate=product_cost(steps, rank_size),
        name="first_section",
    )(left, right, used, blocks, blocks)


def second_sums(regions, left, right, target, sign, live, norm_factor, owner_count):
    steps = left.shape[0]
    slots, rank_size, width = regions[0].shape
    shape = (owner_count * DIAG_DEV, rank_size, width)
    owned = (DIAG_DEV, rank_size, width)
    kinds = [jnp.bfloat16] * (owner_count - 1) + [jnp.float32]
    return pl.pallas_call(
        lambda *refs: second_kernel(len(regions), norm_factor, *refs),
        in_specs=[pl.BlockSpec(memory_space=pltpu.SMEM)] * 5
        + [pl.BlockSpec(memory_space=pl.ANY)] * len(regions),
        out_specs=[pl.BlockSpec(memory_space=pltpu.VMEM)] * owner_count,
        scratch_shapes=[
            pltpu.VMEM((len(regions) * slots, rank_size, width), jnp.bfloat16),
            pltpu.VMEM(shape, jnp.float32),
            pltpu.VMEM((2 * rank_size, width), jnp.bfloat16),
            pltpu.SemaphoreType.DMA((len(regions),)),
        ],
        out_shape=[jax.ShapeDtypeStruct(owned, kind) for kind in kinds],
        compiler_params=pltpu.CompilerParams(vmem_limit_bytes=VMEM_BYTES),
        cost_estimate=product_cost(steps, rank_size),
        name="second_section",
    )(left, right, target, sign, live, *regions)


def source_ranks(sources):
    length = sources.shape[-1]
    positions = jnp.arange(length)
    earlier = positions[:, None] > positions[None, :]
    same_source = sources[..., :, None] == sources[..., None, :]
    return jnp.sum(jnp.logical_and(same_source, earlier), axis=-1)


def pick(table, index):
    match = index[..., None] == jnp.arange(table.shape[0])
    return jnp.sum(jnp.where(match, table, 0), axis=-1)


def body(
    node_blocks,
    first_pulls,
    first_left,
    first_right,
    first_live,
    second_pulls,
    second_left,
    second_right,
    second_live,
    diagram_ids,
    diagram_signs,
):
    group_count = lax.axis_size("ops")
    time_index = lax.axis_index("tm")
    group_index = lax.axis_index("ops")
    worker = time_index * group_count + group_index
    held_nodes = node_blocks.shape[0]
    rank_size = node_blocks.shape[1]
    norm_factor = 1.0 / math.sqrt(2.0 * rank_size)
    first_cap = first_left.shape[1]
    second_reads = second_pulls.shape[1]
    second_cap = second_left.shape[1]
    second_slots = max(1, second_reads // group_count)
    half = group_count // 2

    def far_of(group):
        return 0 if group >= half else group_count - 1

    far_index = jnp.where(group_index >= half, 0, group_count - 1)
    near_rows = lax.all_gather(node_blocks, "tm", axis=0, tiled=True)
    cuts = 2 if held_nodes % 2 == 0 else 1
    pieces = jnp.split(node_blocks, cuts, axis=0)
    chains = [[] for _ in range(cuts)]
    for cut in range(cuts):
        came = lax.ppermute(pieces[cut], "ops", [(0, half), (group_count - 1, half - 1)])
        chains[cut].append(came)
    for step in range(1, half):
        onward = [(half + step - 1, half + step), (half - step, half - 1 - step)]
        for cut in range(cuts):
            chains[cut].append(lax.ppermute(chains[cut][-1], "ops", onward))
    hop = jnp.where(group_index >= half, group_index - half, half - 1 - group_index)

    def arrived_at(chain):
        block = chain[0]
        for step in range(1, half):
            block = jnp.where(hop == step, chain[step], block)
        return block

    far_nodes = jnp.concatenate([arrived_at(chain) for chain in chains], axis=0)
    far_rows = lax.all_gather(far_nodes, "tm", axis=0, tiled=True)

    def own_rows(table):
        return lax.dynamic_slice_in_dim(table, time_index * group_count, group_count, 0)

    def turned(rows):
        return lax.dynamic_slice_in_dim(
            jnp.concatenate([rows, rows], axis=0), group_index, group_count, 0
        )

    row_start = time_index * group_count
    row_pulls = own_rows(second_pulls)
    row_sources = row_pulls // first_cap % group_count
    row_pairs = row_pulls % first_cap
    ranks = source_ranks(row_sources)
    live = jnp.arange(second_cap)[None, :] < own_rows(second_live)[:, None]
    spots = jnp.arange(second_reads)[None, None, :]
    read = jnp.logical_or(
        own_rows(second_left)[:, :, None] == spots, own_rows(second_right)[:, :, None] == spots
    )
    read = jnp.any(jnp.logical_and(read, live[:, :, None]), axis=1)
    slot_ids = jnp.arange(second_slots)[None, :, None]

    def slots_of(sources, source, pairs, slot_ranks, reads):
        chosen = jnp.logical_and((sources == source)[:, None, :], slot_ranks[:, None, :] == slot_ids)
        pair_ids = jnp.sum(jnp.where(chosen, pairs[:, None, :], 0), axis=-1)
        used = jnp.any(jnp.logical_and(chosen, reads[:, None, :]), axis=-1)
        return pair_ids, used.astype(jnp.int32)

    def factors(holder, pair_ids):
        pulls = first_pulls[holder]
        column_pos = pulls // held_nodes // group_count * held_nodes + pulls % held_nodes
        return (
            pick(column_pos, pick(first_left[holder], pair_ids)),
            pick(column_pos, pick(first_right[holder], pair_ids)),
        )

    pair_ids, used = slots_of(
        turned(row_sources), group_index, turned(row_pairs), turned(ranks), turned(read)
    )
    readers = (group_index + jnp.arange(group_count)) % group_count
    apart = jnp.where(readers >= half, 0, group_count - 1) == group_index
    used = jnp.where(apart[:, None], 0, used)
    left_nodes, right_nodes = factors(worker, pair_ids)

    def own_row(rows):
        return lax.dynamic_slice_in_dim(rows, group_index, 1, 0)

    own_sources = own_row(row_sources)
    far_ids, far_used = slots_of(
        own_sources, far_index, own_row(row_pairs), own_row(ranks), own_row(read)
    )
    far_left, far_right = factors(row_start + far_index, far_ids)
    region = jnp.where(
        own_sources == far_index,
        group_count,
        (group_index - own_sources + group_count) % group_count,
    )
    places = (region * second_slots + own_row(ranks))[0]
    second_left_at = pick(places, second_left[worker])
    second_right_at = pick(places, second_right[worker])
    row_targets = diagram_ids[worker] - row_start * DIAG_DEV
    owners = row_targets // DIAG_DEV
    mirrored = jnp.where(group_index >= half, group_count - 1 - owners, owners)
    inner = jnp.where(group_index >= half, group_count - 1 - group_index, group_index)
    if group_count == 4:
        owner_place = jnp.where(mirrored >= 2, 3 - mirrored, jnp.where(mirrored == inner, 3, 2))
    else:
        owner_place = (owners - group_index - 1 + group_count) % group_count
    targets = owner_place * DIAG_DEV + row_targets % DIAG_DEV

    def near_products(turn):
        return first_products(
            near_rows, left_nodes[turn], right_nodes[turn], used[turn], norm_factor
        )

    regions = [None] * (group_count + 1)
    for turn in sorted(range(1, group_count), key=lambda j: -min(j, group_count - j)):
        pairs = [
            (source, (source + turn) % group_count)
            for source in range(group_count)
            if far_of((source + turn) % group_count) != source
        ]
        if pairs:
            regions[turn] = lax.ppermute(near_products(turn), "ops", pairs)
    regions[0] = near_products(0)
    regions[group_count] = first_products(
        far_rows, far_left[0], far_right[0], far_used[0], norm_factor
    )
    regions = [regions[0] if block is None else block for block in regions]
    sums = second_sums(
        regions,
        second_left_at,
        second_right_at,
        targets,
        diagram_signs[worker],
        second_live[worker][None],
        norm_factor,
        group_count,
    )
    result = sums[-1]
    if group_count == 4:
        inward = [(0, 1), (3, 2)]
        end_came = lax.ppermute(sums[0], "ops", inward)
        inner_came = lax.ppermute(sums[1], "ops", inward)
        partner = lax.ppermute(sums[2], "ops", [(0, 1), (1, 0), (2, 3), (3, 2)])
        to_end = sums[0].astype(jnp.float32) + end_came.astype(jnp.float32)
        to_inner = sums[1].astype(jnp.float32) + inner_came.astype(jnp.float32)
        at_end = lax.ppermute(to_end.astype(jnp.bfloat16), "ops", [(1, 3), (2, 0)])
        at_inner = lax.ppermute(to_inner.astype(jnp.bfloat16), "ops", [(1, 2), (2, 1)])
        came = [partner, at_end, at_inner]
    else:
        came = [
            lax.ppermute(
                sums[turn - 1], "ops", [(g, (g + turn) % group_count) for g in range(group_count)]
            )
            for turn in range(1, group_count)
        ]
    for block in came:
        result = result + block.astype(jnp.float32)
    return result


def solution(mesh):
    placed = (P(("tm", "ops"), None, None), P(), P(), P(), P(), P(), P(), P(), P(), P(), P())
    return jax.shard_map(
        body, mesh=mesh, in_specs=placed, out_specs=P(("tm", "ops"), None, None), check_vma=False
    )
```

```python
import math

import jax
import jax.numpy as jnp
from jax import lax
from jax.experimental import pallas as pl
from jax.experimental.pallas import tpu as pltpu
from jax.sharding import PartitionSpec as P

DIAG_DEV = 1
VMEM_BYTES = 48 * 1024 * 1024


def complex_product(first_block, second_block, stacked):
    rank_size = first_block.shape[0]
    stacked[:rank_size, :] = second_block
    stacked[rank_size:, :rank_size] = -second_block[:, rank_size:]
    stacked[rank_size:, rank_size:] = second_block[:, :rank_size]
    return jnp.dot(first_block, stacked[...], preferred_element_type=jnp.float32)


def first_kernel(norm_factor, left, right, used, a_ref, b_ref, out_ref, stacked):
    @pl.when(used[pl.program_id(0)] > 0)
    def _():
        product = complex_product(a_ref[0], b_ref[0], stacked)
        out_ref[0] = (product * norm_factor).astype(out_ref.dtype)


def second_kernel(region_count, norm, left, right, target, sign, live, *refs):
    regions = refs[:region_count]
    *out_refs, held, total, stacked, arrivals = refs[region_count:]
    slots = regions[0].shape[0]
    copies = [
        pltpu.make_async_copy(regions[k], held.at[pl.ds(k * slots, slots)], arrivals.at[k])
        for k in range(region_count)
    ]
    for copy in copies:
        copy.start()
    total[...] = jnp.zeros_like(total)
    for copy in copies:
        copy.wait()

    @pl.loop(0, live[0])
    def _(step):
        weight = sign[step].astype(jnp.float32) * norm
        product = complex_product(held[left[step]], held[right[step]], stacked)
        total[target[step]] += product * weight

    owned = total.shape[0] // len(out_refs)
    for k, out_ref in enumerate(out_refs):
        out_ref[...] = total[pl.ds(k * owned, owned)].astype(out_ref.dtype)


def product_cost(count, rank_size):
    return pl.CostEstimate(
        flops=16 * count * rank_size**3 // 2,
        bytes_accessed=12 * count * rank_size**2,
        transcendentals=0,
    )


def first_products(blocks, left, right, used, norm_factor):
    steps = left.shape[0]
    rank_size = blocks.shape[1]
    block = (1, rank_size, 2 * rank_size)
    return pl.pallas_call(
        lambda *refs: first_kernel(norm_factor, *refs),
        grid_spec=pltpu.PrefetchScalarGridSpec(
            num_scalar_prefetch=3,
            grid=(steps,),
            in_specs=[
                pl.BlockSpec(block, lambda s, left, right, used: (left[s], 0, 0)),
                pl.BlockSpec(block, lambda s, left, right, used: (right[s], 0, 0)),
            ],
            out_specs=pl.BlockSpec(block, lambda s, *_: (s, 0, 0)),
            scratch_shapes=[pltpu.VMEM((2 * rank_size, 2 * rank_size), jnp.bfloat16)],
        ),
        out_shape=jax.ShapeDtypeStruct((steps,) + block[1:], jnp.bfloat16),
        compiler_params=pltpu.CompilerParams(vmem_limit_bytes=VMEM_BYTES),
        cost_estimate=product_cost(steps, rank_size),
        name="first_section",
    )(left, right, used, blocks, blocks)


def second_sums(regions, left, right, target, sign, live, norm_factor, owner_count):
    steps = left.shape[0]
    slots, rank_size, width = regions[0].shape
    shape = (owner_count * DIAG_DEV, rank_size, width)
    owned = (DIAG_DEV, rank_size, width)
    kinds = [jnp.bfloat16] * (owner_count - 1) + [jnp.float32]
    return pl.pallas_call(
        lambda *refs: second_kernel(len(regions), norm_factor, *refs),
        in_specs=[pl.BlockSpec(memory_space=pltpu.SMEM)] * 5
        + [pl.BlockSpec(memory_space=pl.ANY)] * len(regions),
        out_specs=[pl.BlockSpec(memory_space=pltpu.VMEM)] * owner_count,
        scratch_shapes=[
            pltpu.VMEM((len(regions) * slots, rank_size, width), jnp.bfloat16),
            pltpu.VMEM(shape, jnp.float32),
            pltpu.VMEM((2 * rank_size, width), jnp.bfloat16),
            pltpu.SemaphoreType.DMA((len(regions),)),
        ],
        out_shape=[jax.ShapeDtypeStruct(owned, kind) for kind in kinds],
        compiler_params=pltpu.CompilerParams(vmem_limit_bytes=VMEM_BYTES),
        cost_estimate=product_cost(steps, rank_size),
        name="second_section",
    )(left, right, target, sign, live, *regions)


def source_ranks(sources):
    length = sources.shape[-1]
    positions = jnp.arange(length)
    earlier = positions[:, None] > positions[None, :]
    same_source = sources[..., :, None] == sources[..., None, :]
    return jnp.sum(jnp.logical_and(same_source, earlier), axis=-1)


def pick(table, index):
    match = index[..., None] == jnp.arange(table.shape[0])
    return jnp.sum(jnp.where(match, table, 0), axis=-1)


def body(
    node_blocks,
    first_pulls,
    first_left,
    first_right,
    first_live,
    second_pulls,
    second_left,
    second_right,
    second_live,
    diagram_ids,
    diagram_signs,
):
    group_count = lax.axis_size("ops")
    time_index = lax.axis_index("tm")
    group_index = lax.axis_index("ops")
    worker = time_index * group_count + group_index
    held_nodes = node_blocks.shape[0]
    rank_size = node_blocks.shape[1]
    norm_factor = 1.0 / math.sqrt(2.0 * rank_size)
    first_cap = first_left.shape[1]
    second_reads = second_pulls.shape[1]
    second_cap = second_left.shape[1]
    second_slots = max(1, second_reads // group_count)
    half = group_count // 2

    def far_of(group):
        return 0 if group >= half else group_count - 1

    far_index = jnp.where(group_index >= half, 0, group_count - 1)
    near_rows = lax.all_gather(node_blocks, "tm", axis=0, tiled=True)
    cuts = 2 if held_nodes % 2 == 0 else 1
    pieces = jnp.split(node_blocks, cuts, axis=0)
    chains = [[] for _ in range(cuts)]
    for cut in range(cuts):
        came = lax.ppermute(pieces[cut], "ops", [(0, half), (group_count - 1, half - 1)])
        chains[cut].append(came)
    for step in range(1, half):
        onward = [(half + step - 1, half + step), (half - step, half - 1 - step)]
        for cut in range(cuts):
            chains[cut].append(lax.ppermute(chains[cut][-1], "ops", onward))
    hop = jnp.where(group_index >= half, group_index - half, half - 1 - group_index)

    def arrived_at(chain):
        block = chain[0]
        for step in range(1, half):
            block = jnp.where(hop == step, chain[step], block)
        return block

    far_nodes = jnp.concatenate([arrived_at(chain) for chain in chains], axis=0)
    far_rows = lax.all_gather(far_nodes, "tm", axis=0, tiled=True)

    def own_rows(table):
        return lax.dynamic_slice_in_dim(table, time_index * group_count, group_count, 0)

    def turned(rows):
        return lax.dynamic_slice_in_dim(
            jnp.concatenate([rows, rows], axis=0), group_index, group_count, 0
        )

    row_start = time_index * group_count
    row_pulls = own_rows(second_pulls)
    row_sources = row_pulls // first_cap % group_count
    row_pairs = row_pulls % first_cap
    ranks = source_ranks(row_sources)
    live = jnp.arange(second_cap)[None, :] < own_rows(second_live)[:, None]
    spots = jnp.arange(second_reads)[None, None, :]
    read = jnp.logical_or(
        own_rows(second_left)[:, :, None] == spots, own_rows(second_right)[:, :, None] == spots
    )
    read = jnp.any(jnp.logical_and(read, live[:, :, None]), axis=1)
    slot_ids = jnp.arange(second_slots)[None, :, None]

    def slots_of(sources, source, pairs, slot_ranks, reads):
        chosen = jnp.logical_and((sources == source)[:, None, :], slot_ranks[:, None, :] == slot_ids)
        pair_ids = jnp.sum(jnp.where(chosen, pairs[:, None, :], 0), axis=-1)
        used = jnp.any(jnp.logical_and(chosen, reads[:, None, :]), axis=-1)
        return pair_ids, used.astype(jnp.int32)

    def factors(holder, pair_ids):
        pulls = first_pulls[holder]
        column_pos = pulls // held_nodes // group_count * held_nodes + pulls % held_nodes
        return (
            pick(column_pos, pick(first_left[holder], pair_ids)),
            pick(column_pos, pick(first_right[holder], pair_ids)),
        )

    pair_ids, used = slots_of(
        turned(row_sources), group_index, turned(row_pairs), turned(ranks), turned(read)
    )
    readers = (group_index + jnp.arange(group_count)) % group_count
    apart = jnp.where(readers >= half, 0, group_count - 1) == group_index
    used = jnp.where(apart[:, None], 0, used)
    left_nodes, right_nodes = factors(worker, pair_ids)

    def own_row(rows):
        return lax.dynamic_slice_in_dim(rows, group_index, 1, 0)

    own_sources = own_row(row_sources)
    far_ids, far_used = slots_of(
        own_sources, far_index, own_row(row_pairs), own_row(ranks), own_row(read)
    )
    far_left, far_right = factors(row_start + far_index, far_ids)
    region = jnp.where(
        own_sources == far_index,
        group_count,
        (group_index - own_sources + group_count) % group_count,
    )
    places = (region * second_slots + own_row(ranks))[0]
    second_left_at = pick(places, second_left[worker])
    second_right_at = pick(places, second_right[worker])
    row_targets = diagram_ids[worker] - row_start * DIAG_DEV
    owners = row_targets // DIAG_DEV
    mirrored = jnp.where(group_index >= half, group_count - 1 - owners, owners)
    inner = jnp.where(group_index >= half, group_count - 1 - group_index, group_index)
    if group_count == 4:
        owner_place = jnp.where(mirrored >= 2, 3 - mirrored, jnp.where(mirrored == inner, 3, 2))
    else:
        owner_place = (owners - group_index - 1 + group_count) % group_count
    targets = owner_place * DIAG_DEV + row_targets % DIAG_DEV

    def near_products(turn):
        return first_products(
            near_rows, left_nodes[turn], right_nodes[turn], used[turn], norm_factor
        )

    regions = [None] * (group_count + 1)
    for turn in sorted(range(1, group_count), key=lambda j: min(j, group_count - j)):
        pairs = [
            (source, (source + turn) % group_count)
            for source in range(group_count)
            if far_of((source + turn) % group_count) != source
        ]
        if pairs:
            regions[turn] = lax.ppermute(near_products(turn), "ops", pairs)
    regions[0] = near_products(0)
    regions[group_count] = first_products(
        far_rows, far_left[0], far_right[0], far_used[0], norm_factor
    )
    regions = [regions[0] if block is None else block for block in regions]
    sums = second_sums(
        regions,
        second_left_at,
        second_right_at,
        targets,
        diagram_signs[worker],
        second_live[worker][None],
        norm_factor,
        group_count,
    )
    result = sums[-1]
    if group_count == 4:
        inward = [(0, 1), (3, 2)]
        end_came = lax.ppermute(sums[0], "ops", inward)
        inner_came = lax.ppermute(sums[1], "ops", inward)
        partner = lax.ppermute(sums[2], "ops", [(0, 1), (1, 0), (2, 3), (3, 2)])
        to_end = sums[0].astype(jnp.float32) + end_came.astype(jnp.float32)
        to_inner = sums[1].astype(jnp.float32) + inner_came.astype(jnp.float32)
        at_end = lax.ppermute(to_end.astype(jnp.bfloat16), "ops", [(1, 3), (2, 0)])
        at_inner = lax.ppermute(to_inner.astype(jnp.bfloat16), "ops", [(1, 2), (2, 1)])
        came = [partner, at_end, at_inner]
    else:
        came = [
            lax.ppermute(
                sums[turn - 1], "ops", [(g, (g + turn) % group_count) for g in range(group_count)]
            )
            for turn in range(1, group_count)
        ]
    for block in came:
        result = result + block.astype(jnp.float32)
    return result


def solution(mesh):
    placed = (P(("tm", "ops"), None, None), P(), P(), P(), P(), P(), P(), P(), P(), P(), P())
    return jax.shard_map(
        body, mesh=mesh, in_specs=placed, out_specs=P(("tm", "ops"), None, None), check_vma=False
    )
```
